32 devices in a mesh: req: 8 (over z, x), mlp: 4 (over y, core).
Axes of the slice: x: 2, y: 2, z: 4, core: 2. Of those that a mesh axis runs over, the one named last changes fastest.
Arguments:
- x_pages: bfloat16 [256, 8, 4096], P('req', None, 'mlp'), may hold values from -6 to 6
- page_owner: int32 [256], P('req'), may hold values from 0 to 7, as said below
- request_id: int32 [2048], P('req'), may hold values from 0 to 2047, as said below
- adapter_table: int32 [2048], P('req'), may hold values from 0 to 63
- ln_gain: float32 [4096], replicated, may hold values from 0.5 to 1.5
- ln_bias: float32 [4096], replicated, may hold values from -3 to 3
- w_query: bfloat16 [4096, 2048], P('req', 'mlp'), may hold values from -0.09375 to 0.09375
- w_key: bfloat16 [4096, 2048], P('req', 'mlp'), may hold values from -0.09375 to 0.09375
- w_value: bfloat16 [4096, 2048], P('req', 'mlp'), may hold values from -0.09375 to 0.09375
- w_attn_out: bfloat16 [2048, 4096], P('mlp', 'req'), may hold values from -0.125 to 0.125
- down_query: bfloat16 [4096, 1024], P('mlp'), may hold values from -0.09375 to 0.09375
- up_query: bfloat16 [1024, 2048], P(None, 'mlp'), may hold values from -1.5 to 1.5
- down_value: bfloat16 [4096, 1024], P('mlp'), may hold values from -0.09375 to 0.09375
- up_value: bfloat16 [1024, 2048], P(None, 'mlp'), may hold values from -1.5 to 1.5
- w_fc_in: bfloat16 [4096, 8192], P('req', 'mlp'), may hold values from -0.09375 to 0.09375
- b_fc_in: float32 [8192], P('mlp'), may hold values from -3 to 3
- down_fc: bfloat16 [4096, 1024], P('mlp'), may hold values from -0.09375 to 0.09375
- up_fc: bfloat16 [1024, 8192], P(None, 'mlp'), may hold values from -1.5 to 1.5
- w_fc_out: bfloat16 [8192, 4096], P('mlp', 'req'), may hold values from -0.0625 to 0.0625
- b_fc_out: float32 [4096], P('mlp'), may hold values from -3 to 3
Outputs:
- out_pages: bfloat16 [256, 8, 4096], P('req', None, 'mlp')
The draws below stay inside these ranges and needn't reach their ends.
Inputs may be any that keep to these rules, and one draw needn't show every extreme that they name: `page_owner`: every owner receives exactly 32 pages, at most 5 of them from one device, and some device sends exactly 5 pages to some owner. `request_id`: ids never fall; every request lies inside one owner's block of 256 rows, and the ids of block k lie in k * 256 to k * 256 + 255; some request is 256 long.
All inputs are finite; a program needn't handle non-finite values.
Results may differ from the reference program's by a relative error of at most 0.006.
Values may be sent and summed in bfloat16 or wider, within the bound.
A program may use at most 128 MiB of HBM per device.

```python
import math
import jax
import jax.numpy as jnp
import numpy as np
from jax import lax

D = 4096
HEADS = 8
HS = 256
ROT = 64
FF = 8192
NAD = 64
R = 16
PAGE = 8
TOK_DEV = 256
HW = 2048
PG_DEV = 32
PAGES = 256
TOKENS = 2048
N_REQ = 8


def draw_request_id(key, part):
    blocks = TOKENS // TOK_DEV
    key_level = jax.random.fold_in(key, 11)
    key_flag = jax.random.fold_in(key, 12)
    key_long = jax.random.fold_in(key, 13)
    level = jax.random.randint(key_level, (blocks, 1), 1, 5)
    period = jnp.power(4, level).astype(jnp.int32)
    raw = jax.random.randint(key_flag, (blocks, TOK_DEV), 0, 1 << 20)
    flags = (raw % period == 0).astype(jnp.int32)
    column = jnp.arange(TOK_DEV)[None, :]
    long_block = jax.random.randint(key_long, (), 0, blocks)
    flags = jnp.where(column == 0, 1, flags)
    flags = jnp.where((jnp.arange(blocks)[:, None] == long_block) & (column > 0), 0, flags)
    ids = jnp.cumsum(flags, axis=1) - 1 + jnp.arange(blocks)[:, None] * TOK_DEV
    return ids.reshape(-1).astype(jnp.int32)


def draw_page_owner(key, part):
    groups = N_REQ
    per = PG_DEV
    base = per // groups
    key_sign = jax.random.fold_in(key, 21)
    key_rows = jax.random.fold_in(key, 22)
    signs = jnp.where(jax.random.permutation(key_sign, groups) < groups // 2, 1, -1).astype(jnp.int32)
    residue = jnp.arange(groups)

    def one_source(source):
        counts = base + signs[(residue + 2 * source) % groups]
        offsets = jnp.repeat(residue, counts, total_repeat_length=per)
        shuffle = jax.random.permutation(jax.random.fold_in(key_rows, source), per)
        return ((source + offsets[shuffle]) % groups).astype(jnp.int32)
    owners = jax.vmap(one_source)(jnp.arange(groups))
    return owners.reshape(-1).astype(jnp.int32)


def set_ends(drawn, key, smallest, high):
    place = [jax.random.randint(jax.random.fold_in(key, axis), (), 0, length) for axis, length in enumerate(drawn.shape)]
    longest = drawn.shape.index(max(drawn.shape))
    neighbour = place[:longest] + [(place[longest] + 1) % drawn.shape[longest]] + place[longest + 1:]
    return drawn.at[tuple(place)].set(smallest).at[tuple(neighbour)].set(high)


def level_of(rng, shape, pieces, smallest, high):
    factor_of, own = 1.0, jax.random.fold_in(rng, 6)
    for dim, shards_of in pieces:
        draws = jnp.exp(jax.random.uniform(jax.random.fold_in(own, dim), (shards_of,), jnp.float32, smallest / len(pieces), high / len(pieces)))
        factor_of = factor_of * jnp.repeat(draws, shape[dim] // shards_of).reshape([-1 if axis == dim else 1 for axis in range(len(shape))])
    return factor_of


def rank_bounds(count, lean):
    loads = [(1 << 20) // math.isqrt(grade ** lean) + 1 for grade in range(1, count + 1)]
    width = 1 + sum(loads) // (1 << 30)
    return np.cumsum(np.array([max(1, weight // width) for weight in loads]))


def skewed_ids(key, extent, count, skew):
    listing = rank_bounds(count, skew)
    ticket = jax.random.randint(jax.random.fold_in(key, 1), extent, 0, int(listing[count - 1]))
    standing = jnp.searchsorted(jnp.asarray(listing, jnp.int32), ticket, side="right")
    return jax.random.permutation(jax.random.fold_in(key, 2), count)[standing].astype(jnp.int32)


def noise(stream_key, shape, deviation, bound, split=(), kind=jnp.bfloat16):
    drawn = jax.random.normal(stream_key, shape, jnp.float32) * deviation
    if len(split) > 0:
        drawn = level_of(stream_key, shape, split, -0.22, 0.18) * drawn
    return jnp.clip(drawn, min=-bound, max=bound).astype(kind)


def setup_inputs(seed: int = 0) -> dict:
    arg_keys = jax.random.split(jax.random.key(seed), 21)
    return {
        "x_pages": noise(arg_keys[0], (PAGES, PAGE, D), 1.0, 6.0, ((0, 8), (2, 4))),
        "page_owner": draw_page_owner(jax.random.fold_in(arg_keys[20], 71), 0),
        "request_id": draw_request_id(jax.random.fold_in(arg_keys[20], 71), 0),
        "adapter_table": set_ends(skewed_ids(arg_keys[3], (TOKENS,), NAD, 2), jax.random.fold_in(arg_keys[3], 3), 0, NAD - 1).astype(jnp.int32),
        "ln_gain": jnp.clip(1.0 + 0.1 * jax.random.normal(arg_keys[4], (D,), jnp.float32), 0.5, 1.5),
        "ln_bias": noise(arg_keys[5], (D,), 0.3, 3.0, (), jnp.float32),
        "w_query": noise(arg_keys[6], (D, HW), D ** -0.5, 0.09375, ((0, 8), (1, 4))),
        "w_key": noise(arg_keys[7], (D, HW), D ** -0.5, 0.09375, ((0, 8), (1, 4))),
        "w_value": noise(arg_keys[8], (D, HW), D ** -0.5, 0.09375, ((0, 8), (1, 4))),
        "w_attn_out": noise(arg_keys[9], (HW, D), HW ** -0.5, 0.125, ((0, 4), (1, 8))),
        "down_query": noise(arg_keys[10], (D, NAD * R), D ** -0.5, 0.09375, ((0, 4),)),
        "up_query": noise(arg_keys[11], (NAD * R, HW), R ** -0.5, 1.5, ((1, 4),)),
        "down_value": noise(arg_keys[12], (D, NAD * R), D ** -0.5, 0.09375, ((0, 4),)),
        "up_value": noise(arg_keys[13], (NAD * R, HW), R ** -0.5, 1.5, ((1, 4),)),
        "w_fc_in": noise(arg_keys[14], (D, FF), D ** -0.5, 0.09375, ((0, 8), (1, 4))),
        "b_fc_in": noise(arg_keys[15], (FF,), 0.5, 3.0, ((0, 4),), jnp.float32),
        "down_fc": noise(arg_keys[16], (D, NAD * R), D ** -0.5, 0.09375, ((0, 4),)),
        "up_fc": noise(arg_keys[17], (NAD * R, FF), R ** -0.5, 1.5, ((1, 4),)),
        "w_fc_out": noise(arg_keys[18], (FF, D), FF ** -0.5, 0.0625, ((0, 4), (1, 8))),
        "b_fc_out": noise(arg_keys[19], (D,), 0.5, 3.0, ((0, 4),), jnp.float32),
    }


EPS = 1e-05

def gelu_tanh(v):
    return 0.5 * v * (1.0 + jnp.tanh(0.7978845608028654 * (v + 0.044715 * v * v * v)))

def rotate(block, pos):
    half = ROT // 2
    freq = jnp.power(10000.0, -jnp.arange(half).astype(jnp.float32) * 2.0 / ROT)
    angle = pos.astype(jnp.float32)[:, None, None] * freq[None, None, :]
    cosine = jnp.cos(angle)
    sine = jnp.sin(angle)
    even = block[:, :, 0:ROT:2]
    odd = block[:, :, 1:ROT:2]
    turned = jnp.stack([even * cosine - odd * sine, odd * cosine + even * sine], axis=-1)
    turned = turned.reshape(block.shape[0], block.shape[1], ROT)
    return jnp.concatenate([turned, block[:, :, ROT:]], axis=2)

def low_rank(normed, down, up, onehot):
    rows = normed.shape[0]
    spread = jnp.dot(normed, down, preferred_element_type=jnp.float32).reshape(rows, NAD, R)
    chosen = lax.optimization_barrier(jnp.sum(spread * onehot[:, :, None], axis=1)).astype(jnp.bfloat16)
    expanded = (onehot.astype(jnp.bfloat16)[:, :, None] * chosen[:, None, :]).reshape(rows, NAD * R)
    return jnp.dot(expanded, up, preferred_element_type=jnp.float32)

def reference(x_pages, page_owner, request_id, adapter_table, ln_gain, ln_bias, w_query, w_key, w_value, w_attn_out, down_query, up_query, down_value, up_value, w_fc_in, b_fc_in, down_fc, up_fc, w_fc_out, b_fc_out):
    order = jnp.argsort(page_owner, stable=True).astype(jnp.int32)
    moved = x_pages[order].reshape(N_REQ, TOK_DEV, D)
    owner_ids = request_id.reshape(N_REQ, TOK_DEV)

    def layer(item):
        rows, ids = item
        count = rows.shape[0]
        xf = rows.astype(jnp.float32)
        mean = lax.optimization_barrier(jnp.mean(xf, axis=1, keepdims=True))
        var = lax.optimization_barrier(jnp.mean(jnp.square(xf - mean), axis=1, keepdims=True))
        normed = ((xf - mean) * lax.rsqrt(var + EPS) * ln_gain + ln_bias).astype(jnp.bfloat16)
        adapter = adapter_table[ids]
        onehot = (adapter[:, None] == jnp.arange(NAD)[None, :]).astype(jnp.float32)
        index = jnp.arange(count)
        start = lax.optimization_barrier(jnp.sum((ids[None, :] < ids[:, None]).astype(jnp.int32), axis=1))
        pos = index - start
        query = jnp.dot(normed, w_query, preferred_element_type=jnp.float32) + low_rank(normed, down_query, up_query, onehot)
        keys = jnp.dot(normed, w_key, preferred_element_type=jnp.float32)
        value = (jnp.dot(normed, w_value, preferred_element_type=jnp.float32) + low_rank(normed, down_value, up_value, onehot)).astype(jnp.bfloat16)
        query = rotate(query.reshape(count, HEADS, HS), pos).astype(jnp.bfloat16)
        keys = rotate(keys.reshape(count, HEADS, HS), pos).astype(jnp.bfloat16)
        value = value.reshape(count, HEADS, HS)
        mask = (ids[:, None] == ids[None, :]) & (index[None, :] <= index[:, None])
        scores = jnp.einsum('qhd,khd->hqk', query.astype(jnp.float32), keys.astype(jnp.float32)) * HS ** (-0.5)
        scores = jnp.where(mask[None, :, :], scores, -1e+30)
        top = lax.optimization_barrier(jnp.max(scores, axis=2, keepdims=True))
        weights = jnp.exp(scores - top)
        probs = (weights / lax.optimization_barrier(jnp.sum(weights, axis=2, keepdims=True))).astype(jnp.bfloat16)
        attn = jnp.einsum('hqk,khd->qhd', probs.astype(jnp.float32), value.astype(jnp.float32)).astype(jnp.bfloat16).reshape(count, HW)
        hidden_pre = jnp.dot(normed, w_fc_in, preferred_element_type=jnp.float32) + low_rank(normed, down_fc, up_fc, onehot) + b_fc_in
        hidden = gelu_tanh(hidden_pre).astype(jnp.bfloat16)
        mixed = jnp.dot(attn, w_attn_out, preferred_element_type=jnp.float32) + jnp.dot(hidden, w_fc_out, preferred_element_type=jnp.float32)
        return (xf + mixed + b_fc_out).astype(jnp.bfloat16)
    result = lax.map(layer, (moved, owner_ids))
    back = jnp.argsort(order).astype(jnp.int32)
    return result.reshape(PAGES, PAGE, D)[back]
```

```python
import jax
import jax.numpy as jnp
from jax import lax
from jax.sharding import PartitionSpec as P

HS = 256
ROT = 64
NAD = 64
R = 16
EPS = 1e-05

bf16 = jnp.bfloat16
f32 = jnp.float32


def mm(a, b):
    return jnp.dot(a, b, preferred_element_type=f32)


def gelu_tanh(v):
    return 0.5 * v * (1.0 + jnp.tanh(0.7978845608028654 * (v + 0.044715 * v * v * v)))


def rotate_flat(block, pos):
    cols = block.shape[1]
    within = jnp.arange(cols) % HS
    turned = within < ROT
    freq = jnp.power(10000.0, -(within // 2).astype(f32) * 2.0 / ROT)
    angle = jnp.where(turned[None, :], pos.astype(f32)[:, None] * freq[None, :], 0.0)
    even = (within % 2 == 0)[None, :]
    other = jnp.where(even, -jnp.roll(block, -1, axis=1), jnp.roll(block, 1, axis=1))
    return jnp.where(turned[None, :], block * jnp.cos(angle) + other * jnp.sin(angle), block)


def scatter_sum(part):
    return lax.psum_scatter(part, "req", scatter_dimension=0, tiled=False)


def gather_rows(act):
    return lax.all_gather(act, "req", axis=0, tiled=False)


def on_device(
    x_pages,
    page_owner,
    request_id,
    adapter_table,
    ln_gain,
    ln_bias,
    w_query,
    w_key,
    w_value,
    w_attn_out,
    down_query,
    up_query,
    down_value,
    up_value,
    w_fc_in,
    b_fc_in,
    down_fc,
    up_fc,
    w_fc_out,
    b_fc_out,
):
    groups = lax.axis_size("req")
    lanes = lax.axis_size("mlp")
    me = lax.axis_index("req")
    pg_dev, page_len, width_m = x_pages.shape
    pages = groups * pg_dev
    tok = request_id.shape[0]
    width = width_m * lanes
    chunk = w_query.shape[0]
    heads_w = w_query.shape[1]
    ff = w_fc_in.shape[1]

    local_req = request_id - me * tok
    lookup = local_req[:, None] == jnp.arange(tok)[None, :]
    adapter = jnp.sum(jnp.where(lookup, adapter_table[None, :], 0), axis=1)
    ints = lax.all_gather(jnp.concatenate([page_owner, adapter]), "req", axis=0, tiled=False)
    owner_all = ints[:, :pg_dev].reshape(pages)
    adapter_all = ints[:, pg_dev:].reshape(pages, page_len)
    iota = jnp.arange(pages)
    earlier = (owner_all[None, :] == owner_all[:, None]) & (iota[None, :] < iota[:, None])
    dest = owner_all * pg_dev + jnp.sum(earlier.astype(jnp.int32), axis=1)
    perm = dest[None, :] == iota[:, None]
    perm_low = perm.astype(bf16)
    mine = lax.dynamic_slice_in_dim(dest, me * pg_dev, pg_dev, 0)
    held_adapter = jnp.sum(
        jnp.where((mine[:, None] == iota[None, :])[:, :, None], adapter_all[None, :, :], 0), axis=1
    ).reshape(tok)

    x = x_pages.reshape(tok, width_m).astype(f32)
    local_mean = jnp.mean(x, axis=1)
    local_m2 = jnp.sum(jnp.square(x - local_mean[:, None]), axis=1)
    stats = lax.all_gather(jnp.stack([local_mean, local_m2]), "mlp", axis=0, tiled=False)
    mean = jnp.mean(stats[:, 0], axis=0)
    m2 = jnp.sum(stats[:, 1] + width_m * jnp.square(stats[:, 0] - mean[None, :]), axis=0)
    scale = lax.rsqrt(m2 / width + EPS)
    column = lax.axis_index("mlp") * width_m
    gain = lax.dynamic_slice_in_dim(ln_gain, column, width_m, 0)
    bias = lax.dynamic_slice_in_dim(ln_bias, column, width_m, 0)
    normed = ((x - mean[:, None]) * scale[:, None] * gain + bias).astype(bf16)

    full_rows = lax.all_gather(normed, "mlp", axis=1, tiled=True)
    everyone = lax.all_to_all(full_rows, "req", split_axis=1, concat_axis=0, tiled=True)
    ordered = mm(perm_low, everyone.reshape(pages, page_len * chunk)).astype(bf16)
    ordered = ordered.reshape(groups * tok, chunk)

    col_adapter = jnp.arange(NAD * R) // R
    fold = (jnp.arange(NAD * R)[:, None] % R == jnp.arange(R)[None, :]).astype(bf16)
    held_mask = held_adapter[:, None] == col_adapter[None, :]

    def pick(down):
        return mm(jnp.where(held_mask, mm(normed, down), 0.0).astype(bf16), fold)

    picked = jnp.concatenate([pick(down_query), pick(down_value), pick(down_fc)], axis=1)
    picked = lax.all_gather(picked.astype(bf16), ("req", "mlp"), axis=0, tiled=False)
    picked = jnp.sum(picked.reshape(groups, lanes, tok, 3 * R).astype(f32), axis=1).astype(bf16)
    own_perm = lax.dynamic_slice_in_dim(perm_low, me * pg_dev, pg_dev, 0)
    chosen = mm(own_perm, picked.reshape(pages, page_len * 3 * R)).astype(bf16)
    chosen = chosen.reshape(tok, 3 * R)
    own_mask = adapter[:, None] == col_adapter[None, :]

    def lift(low, up):
        wide = mm(low, fold.T).astype(bf16)
        return mm(jnp.where(own_mask, wide, jnp.zeros((), bf16)), up)

    part = jnp.concatenate(
        [mm(ordered, w).astype(bf16) for w in (w_query, w_key, w_value, w_fc_in)], axis=1
    )
    base = scatter_sum(part.reshape(groups, tok, 3 * heads_w + ff)).astype(f32)

    row_iota = jnp.arange(tok)
    start = jnp.sum((request_id[None, :] < request_id[:, None]).astype(jnp.int32), axis=1)
    pos = row_iota - start
    mask = (request_id[:, None] == request_id[None, :]) & (row_iota[None, :] <= row_iota[:, None])
    query = base[:, :heads_w] + lift(chosen[:, :R], up_query)
    query = rotate_flat(query, pos).astype(bf16).reshape(tok, heads_w // HS, HS)
    keys = rotate_flat(base[:, heads_w : 2 * heads_w], pos).astype(bf16)
    keys = keys.reshape(tok, heads_w // HS, HS)
    value = base[:, 2 * heads_w : 3 * heads_w] + lift(chosen[:, R : 2 * R], up_value)
    value = value.astype(bf16).reshape(tok, heads_w // HS, HS)
    scores = jnp.einsum("qhd,khd->hqk", query, keys, preferred_element_type=f32) * HS ** (-0.5)
    scores = jnp.where(mask[None, :, :], scores, -1e30)
    top = jnp.max(scores, axis=2, keepdims=True)
    weights = jnp.exp(scores - top)
    probs = (weights / jnp.sum(weights, axis=2, keepdims=True)).astype(bf16)
    attn = jnp.einsum("hqk,khd->qhd", probs, value, preferred_element_type=f32)
    attn = attn.astype(bf16).reshape(tok, heads_w)
    hidden = gelu_tanh(base[:, 3 * heads_w :] + lift(chosen[:, 2 * R :], up_fc) + b_fc_in)
    act = jnp.concatenate([attn, hidden.astype(bf16)], axis=1)

    acts = gather_rows(act).reshape(groups * tok, heads_w + ff)
    out = mm(acts[:, :heads_w], w_attn_out) + mm(acts[:, heads_w:], w_fc_out)
    out = out.astype(bf16).reshape(pages, page_len * chunk)
    out = mm(perm_low.T, out).astype(bf16).reshape(groups * tok, chunk)
    shares = lax.all_to_all(out, "req", split_axis=0, concat_axis=1, tiled=True)
    shares = lax.psum_scatter(shares, "mlp", scatter_dimension=1, tiled=True)
    result = (x + shares.astype(f32) + b_fc_out).astype(bf16)
    return result.reshape(pg_dev, page_len, width_m)


def solution(mesh):
    in_specs = (
        P("req", None, "mlp"),
        P("req"),
        P("req"),
        P("req"),
        P(),
        P(),
        P("req", "mlp"),
        P("req", "mlp"),
        P("req", "mlp"),
        P("mlp", "req"),
        P("mlp", None),
        P(None, "mlp"),
        P("mlp", None),
        P(None, "mlp"),
        P("req", "mlp"),
        P("mlp"),
        P("mlp", None),
        P(None, "mlp"),
        P("mlp", "req"),
        P("mlp"),
    )
    out_specs = P("req", None, "mlp")
    return jax.shard_map(
        on_device, mesh=mesh, in_specs=in_specs, out_specs=out_specs, check_vma=False
    )
```

```python
import functools

import jax
import jax.numpy as jnp
from jax import lax
from jax.experimental import pallas as pl
from jax.experimental.pallas import tpu as pltpu
from jax.sharding import PartitionSpec as P

HS = 256
ROT = 64
NAD = 64
R = 16
EPS = 1e-05

bf16 = jnp.bfloat16
f32 = jnp.float32


def mm(a, b):
    return jnp.dot(a, b, preferred_element_type=f32)


def gelu_tanh(v):
    return 0.5 * v * (1.0 + jnp.tanh(0.7978845608028654 * (v + 0.044715 * v * v * v)))


def rotate_flat(block, pos):
    cols = block.shape[1]
    within = jnp.arange(cols) % HS
    turned = within < ROT
    freq = jnp.power(10000.0, -(within // 2).astype(f32) * 2.0 / ROT)
    angle = jnp.where(turned[None, :], pos.astype(f32)[:, None] * freq[None, :], 0.0)
    even = (within % 2 == 0)[None, :]
    other = jnp.where(even, -jnp.roll(block, -1, axis=1), jnp.roll(block, 1, axis=1))
    return jnp.where(turned[None, :], block * jnp.cos(angle) + other * jnp.sin(angle), block)


MESH = pl.DeviceIdType.MESH
VM = pl.BlockSpec(memory_space=pltpu.VMEM)
TILE = 512


def params(collective_id, mib):
    return pltpu.CompilerParams(
        collective_id=collective_id, has_side_effects=True, vmem_limit_bytes=mib << 20
    )


def signal(barrier, target):
    pl.semaphore_signal(barrier, inc=1, device_id=target, device_id_type=MESH)


def ring_place(index, n):
    turn, height = index % 2, index // 2
    return height + turn * (n - 1 - 2 * height)


def ring_index(place, n):
    turn = place // (n // 2)
    return 2 * (place + turn * (n - 1 - 2 * place)) + turn


def ring_ids(n):
    place = ring_place(lax.axis_index("req"), n)
    lane = lax.axis_index("mlp")
    right = (ring_index((place + 1) % n, n), lane)
    left = (ring_index((place + n - 1) % n, n), lane)
    return place, (right, left)


def ring_barrier(targets):
    barrier = pltpu.get_barrier_semaphore()
    for target in targets:
        signal(barrier, target)
    pl.semaphore_wait(barrier, 2)


def reduce_kernel(n, x_ref, w_ref, extra_ref, sum_ref, esum_ref, first, got, egot, sends, recvs):
    half = n // 2
    tiles = w_ref.shape[0]
    rows = x_ref.shape[1]
    mid = rows // 2
    place, targets = ring_ids(n)
    ring_barrier(targets)
    spans = (pl.ds(0, mid), pl.ds(mid, mid))

    def owner(side, step):
        away = half - step if side == 0 else n - half + step
        return ring_index((place + away) % n, n)

    def own(index, t):
        return mm(x_ref[index], w_ref[t])

    def move(side, step, t, extra=False):
        slot = tiles if extra else t
        buffer = egot if extra else got
        if step == 0:
            src = buffer.at[2 * half, spans[side]] if extra else first.at[t, spans[side]]
            at = (side * half, spans[side])
        else:
            at = (side * half + step,)
            src = buffer.at[side * half + step - 1] if extra else got.at[side * half + step - 1, t]
        if not extra:
            at = (at[0], t) + at[1:]
        return pltpu.make_async_remote_copy(
            src_ref=src,
            dst_ref=buffer.at[at],
            send_sem=sends.at[side * half + step, slot],
            recv_sem=recvs.at[side * half + step, slot],
            device_id=targets[side],
            device_id_type=MESH,
        )

    egot[2 * half] = extra_ref[owner(0, 0)]
    for side in (0, 1):
        move(side, 0, 0, True).start()

    @pl.loop(0, tiles)
    def _(t):
        first[t] = own(owner(0, 0), t).astype(bf16)
        for side in (0, 1):
            move(side, 0, t).start()

    for step in range(1, half):
        for side in (0, 1):
            slot = side * half + step - 1
            mine = extra_ref[owner(side, step)]
            move(side, step - 1, 0, True).wait_recv()
            if step == 1:
                egot[slot, spans[side]] += mine[side * mid : side * mid + mid]
                egot[slot, spans[1 - side]] = mine[(1 - side) * mid : (1 - side) * mid + mid]
            else:
                egot[slot] += mine
            move(side, step, 0, True).start()

        @pl.loop(0, tiles)
        def _(t):
            for side in (0, 1):
                slot = side * half + step - 1
                mine = own(owner(side, step), t)
                move(side, step - 1, t).wait_recv()
                if step == 1:
                    a = mine[side * mid : side * mid + mid]
                    b = mine[(1 - side) * mid : (1 - side) * mid + mid]
                    here = got[slot, t, spans[side]].astype(f32)
                    got[slot, t, spans[side]] = (here + a).astype(bf16)
                    got[slot, t, spans[1 - side]] = b.astype(bf16)
                else:
                    got[slot, t] = (got[slot, t].astype(f32) + mine).astype(bf16)
                move(side, step, t).start()

    for side in (0, 1):
        move(side, half - 1, 0, True).wait_recv()
    me = lax.axis_index("req")
    esum_ref[...] = extra_ref[me] + egot[half - 1] + egot[2 * half - 1]

    @pl.loop(0, tiles)
    def _(t):
        mine = own(me, t)
        for side in (0, 1):
            move(side, half - 1, t).wait_recv()
        sum_ref[t] = mine + got[half - 1, t].astype(f32) + got[2 * half - 1, t].astype(f32)

    for step in range(half):
        for side in (0, 1):
            move(side, step, 0, True).wait_send()

        @pl.loop(0, tiles)
        def _(t):
            for side in (0, 1):
                move(side, step, t).wait_send()


def reduce_rows(x, w, extra):
    n, rows, _ = x.shape
    tiles = w.shape[0]
    pad = extra.shape[2]
    return pl.pallas_call(
        functools.partial(reduce_kernel, n),
        out_shape=(
            jax.ShapeDtypeStruct((tiles, rows, TILE), f32),
            jax.ShapeDtypeStruct((rows, pad), bf16),
        ),
        in_specs=[VM] * 3,
        out_specs=(VM, VM),
        scratch_shapes=[
            pltpu.VMEM((tiles, rows, TILE), bf16),
            pltpu.VMEM((n, tiles, rows, TILE), bf16),
            pltpu.VMEM((n + 1, rows, pad), bf16),
            pltpu.SemaphoreType.DMA((n, tiles + 1)),
            pltpu.SemaphoreType.DMA((n, tiles + 1)),
        ],
        compiler_params=params(1, 48),
        name="reduce_rows",
    )(x, w, extra)


def gather_kernel(n, act_ref, w_ref, out_ref, got, total, sends, recvs):
    half = n // 2
    tiles = w_ref.shape[0]
    rows = act_ref.shape[1]
    mid = rows // 2
    place, targets = ring_ids(n)
    ring_barrier(targets)
    spans = (pl.ds(0, mid), pl.ds(mid, mid))

    def move(side, step, t):
        src = act_ref.at[t] if step == 0 else got.at[side * half + step - 1, t]
        dst = got.at[side * half + step, t]
        if step == half - 1:
            dst = got.at[half - 1, t, spans[side]]
            src = src.at[spans[side]]
        return pltpu.make_async_remote_copy(
            src_ref=src,
            dst_ref=dst,
            send_sem=sends.at[side * half + step, t],
            recv_sem=recvs.at[side * half + step, t],
            device_id=targets[side],
            device_id_type=MESH,
        )

    @pl.loop(0, tiles)
    def _(t):
        for side in (0, 1):
            move(side, 0, t).start()

    total[...] = jnp.zeros_like(total)

    @pl.loop(0, tiles)
    def _(t):
        total[0] += mm(act_ref[t], w_ref[t])

    out_ref[lax.axis_index("req")] = total[0].astype(bf16)

    for step in range(1, half):
        total[...] = jnp.zeros_like(total)

        @pl.loop(0, tiles)
        def _(t):
            for side in (0, 1):
                move(side, step - 1, t).wait_recv()
                move(side, step, t).start()
            for side in (0, 1):
                total[side] += mm(got[side * half + step - 1, t], w_ref[t])

        for side in (0, 1):
            away = n - step if side == 0 else step
            out_ref[ring_index((place + away) % n, n)] = total[side].astype(bf16)

    total[...] = jnp.zeros_like(total)

    @pl.loop(0, tiles)
    def _(t):
        for side in (0, 1):
            move(side, half - 1, t).wait_recv()
        total[0] += mm(got[half - 1, t], w_ref[t])

    out_ref[ring_index((place + half) % n, n)] = total[0].astype(bf16)

    for step in range(half):

        @pl.loop(0, tiles)
        def _(t):
            for side in (0, 1):
                move(side, step, t).wait_send()


def gather_multiply(act, w, n):
    tiles, rows, _ = act.shape
    return pl.pallas_call(
        functools.partial(gather_kernel, n),
        out_shape=jax.ShapeDtypeStruct((n, rows, w.shape[2]), bf16),
        in_specs=[VM] * 2,
        out_specs=VM,
        scratch_shapes=[
            pltpu.VMEM((n, tiles, rows, TILE), bf16),
            pltpu.VMEM((2, rows, w.shape[2]), f32),
            pltpu.SemaphoreType.DMA((n, tiles)),
            pltpu.SemaphoreType.DMA((n, tiles)),
        ],
        compiler_params=params(2, 48),
        name="gather_multiply",
    )(act, w)


def exchange_barrier(n, lanes):
    me, lane = lax.axis_index("req"), lax.axis_index("mlp")
    per = n // lanes
    alone = jnp.where(me // per == lane, 1, 0)
    barrier = pltpu.get_barrier_semaphore()
    for k in range(1, lanes):
        signal(barrier, (me, (lane + k) % lanes))

    @pl.loop(0, n)
    def _(i):
        there, t = lane * per + i // lanes, i % lanes

        @pl.when((there != me) | (t != lane))
        def _():
            signal(barrier, (there, t))

        @pl.when((i != me) | (me // per != lane))
        def _():
            signal(barrier, (i, me // per))

    pl.semaphore_wait(barrier, lanes - 1 + 2 * (n - alone))


def spread_kernel(n, lanes, x_ref, pick_ref, all_ref, picks_ref, sends, recvs, msends, mrecvs, ps, pr):
    me, lane = lax.axis_index("req"), lax.axis_index("mlp")
    per = n // lanes
    exchange_barrier(n, lanes)

    def out_move(j, t, source):
        return pltpu.make_async_remote_copy(
            src_ref=x_ref.at[j, t],
            dst_ref=all_ref.at[source, t],
            send_sem=sends.at[j, t],
            recv_sem=recvs.at[source],
            device_id=(lane * per + j, t),
            device_id_type=MESH,
        )

    def in_move(source):
        return pltpu.make_async_remote_copy(
            src_ref=x_ref.at[0, lane],
            dst_ref=all_ref.at[source, lane],
            send_sem=sends.at[0, lane],
            recv_sem=recvs.at[source],
            device_id=(source, me // per),
            device_id_type=MESH,
        )

    def fan(k, source, t):
        return pltpu.make_async_remote_copy(
            src_ref=all_ref.at[source, t],
            dst_ref=all_ref.at[source, t],
            send_sem=msends.at[k, source],
            recv_sem=mrecvs.at[t, source],
            device_id=(me, (lane + k) % lanes),
            device_id_type=MESH,
        )

    def share(k, t):
        return pltpu.make_async_remote_copy(
            src_ref=pick_ref,
            dst_ref=picks_ref.at[t],
            send_sem=ps.at[k],
            recv_sem=pr.at[t],
            device_id=(me, (lane + k) % lanes),
            device_id_type=MESH,
        )

    @pl.loop(0, n)
    def _(i):
        j, t = i // lanes, i % lanes
        self = (lane * per + j == me) & (t == lane)

        @pl.when(jnp.logical_not(self))
        def _():
            out_move(j, t, me).start()

        @pl.when(self)
        def _():
            all_ref[me, lane] = x_ref[j, t]

    for k in range(1, lanes):
        share(k, lane).start()
    picks_ref[lane] = pick_ref[...]

    @pl.loop(0, n)
    def _(i):
        source = (me + i) % n

        @pl.when((source != me) | (me // per != lane))
        def _():
            in_move(source).wait_recv()

        for k in range(1, lanes):
            fan(k, source, lane).start()

    @pl.loop(0, n)
    def _(source):
        for k in range(1, lanes):
            fan(k, source, (lane + k) % lanes).wait_recv()

    for k in range(1, lanes):
        share(k, (lane + k) % lanes).wait_recv()
        share(k, lane).wait_send()

    @pl.loop(0, n)
    def _(i):
        j, t = i // lanes, i % lanes

        @pl.when((lane * per + j != me) | (t != lane))
        def _():
            out_move(j, t, me).wait_send()

        for k in range(1, lanes):
            fan(k, i, lane).wait_send()


def spread_rows(x, picked, n, lanes):
    _, _, part, chunk = x.shape
    return pl.pallas_call(
        functools.partial(spread_kernel, n, lanes),
        out_shape=(
            jax.ShapeDtypeStruct((n, lanes, part, chunk), bf16),
            jax.ShapeDtypeStruct((lanes,) + picked.shape, bf16),
        ),
        in_specs=[VM] * 2,
        out_specs=(VM, VM),
        scratch_shapes=[
            pltpu.SemaphoreType.DMA((n // lanes, lanes)),
            pltpu.SemaphoreType.DMA((n,)),
            pltpu.SemaphoreType.DMA((lanes, n)),
            pltpu.SemaphoreType.DMA((lanes, n)),
            pltpu.SemaphoreType.DMA((lanes,)),
            pltpu.SemaphoreType.DMA((lanes,)),
        ],
        compiler_params=params(3, 24),
        name="spread_rows",
    )(x, picked)


def collect_kernel(n, lanes, y_ref, out_ref, part, ready, msends, mrecvs, sends, recvs):
    me, lane = lax.axis_index("req"), lax.axis_index("mlp")
    per = n // lanes
    exchange_barrier(n, lanes)

    def cross(k, d):
        return pltpu.make_async_remote_copy(
            src_ref=y_ref.at[d, (lane + k) % lanes],
            dst_ref=part.at[k - 1, d],
            send_sem=msends.at[k - 1, d],
            recv_sem=mrecvs.at[k - 1, d],
            device_id=(me, (lane + k) % lanes),
            device_id_type=MESH,
        )

    def home(d):
        return pltpu.make_async_remote_copy(
            src_ref=ready.at[d],
            dst_ref=out_ref.at[me % per, lane],
            send_sem=sends.at[d],
            recv_sem=recvs.at[me % per, lane],
            device_id=(d, me // per),
            device_id_type=MESH,
        )

    def arrive(j, t):
        return pltpu.make_async_remote_copy(
            src_ref=ready.at[0],
            dst_ref=out_ref.at[j, t],
            send_sem=sends.at[0],
            recv_sem=recvs.at[j, t],
            device_id=(lane * per + j, t),
            device_id_type=MESH,
        )

    @pl.loop(0, n)
    def _(i):
        for k in range(1, lanes):
            cross(k, (me + i) % n).start()

    @pl.loop(0, n)
    def _(i):
        d = (me + i) % n
        total = y_ref[d, lane].astype(f32)
        for k in range(1, lanes):
            cross(k, d).wait_recv()
            total += part[k - 1, d].astype(f32)
        ready[d] = total.astype(bf16)
        self = (d == me) & (me // per == lane)

        @pl.when(jnp.logical_not(self))
        def _():
            home(d).start()

        @pl.when(self)
        def _():
            out_ref[me % per, lane] = total.astype(bf16)

    @pl.loop(0, n)
    def _(i):
        j, t = i // lanes, i % lanes

        @pl.when((lane * per + j != me) | (t != lane))
        def _():
            arrive(j, t).wait_recv()

        @pl.when((i != me) | (me // per != lane))
        def _():
            home(i).wait_send()

        for k in range(1, lanes):
            cross(k, i).wait_send()


def collect_rows(y):
    n, lanes, rows, chunk = y.shape
    per = n // lanes
    return pl.pallas_call(
        functools.partial(collect_kernel, n, lanes),
        out_shape=jax.ShapeDtypeStruct((per, lanes, rows, chunk), bf16),
        in_specs=[VM],
        out_specs=VM,
        scratch_shapes=[
            pltpu.VMEM((lanes - 1, n, rows, chunk), bf16),
            pltpu.VMEM((n, rows, chunk), bf16),
            pltpu.SemaphoreType.DMA((lanes - 1, n)),
            pltpu.SemaphoreType.DMA((lanes - 1, n)),
            pltpu.SemaphoreType.DMA((n,)),
            pltpu.SemaphoreType.DMA((per, lanes)),
        ],
        compiler_params=params(4, 24),
        name="collect_rows",
    )(y)


def on_device(
    x_pages,
    page_owner,
    request_id,
    adapter_table,
    ln_gain,
    ln_bias,
    w_query,
    w_key,
    w_value,
    w_attn_out,
    down_query,
    up_query,
    down_value,
    up_value,
    w_fc_in,
    b_fc_in,
    down_fc,
    up_fc,
    w_fc_out,
    b_fc_out,
):
    groups = lax.axis_size("req")
    lanes = lax.axis_size("mlp")
    me = lax.axis_index("req")
    pg_dev, page_len, width_m = x_pages.shape
    pages = groups * pg_dev
    tok = request_id.shape[0]
    width = width_m * lanes
    chunk = w_query.shape[0]
    heads_w = w_query.shape[1]
    ff = w_fc_in.shape[1]

    local_req = request_id - me * tok
    lookup = local_req[:, None] == jnp.arange(tok)[None, :]
    adapter = jnp.sum(jnp.where(lookup, adapter_table[None, :], 0), axis=1)
    ints = lax.all_gather(jnp.concatenate([page_owner, adapter]), "req", axis=0, tiled=False)
    owner_all = ints[:, :pg_dev].reshape(pages)
    adapter_all = ints[:, pg_dev:].reshape(pages, page_len)
    iota = jnp.arange(pages)
    earlier = (owner_all[None, :] == owner_all[:, None]) & (iota[None, :] < iota[:, None])
    dest = owner_all * pg_dev + jnp.sum(earlier.astype(jnp.int32), axis=1)
    perm = dest[None, :] == iota[:, None]
    perm_low = perm.astype(bf16)
    mine = lax.dynamic_slice_in_dim(dest, me * pg_dev, pg_dev, 0)
    held_adapter = jnp.sum(
        jnp.where((mine[:, None] == iota[None, :])[:, :, None], adapter_all[None, :, :], 0), axis=1
    ).reshape(tok)

    x = x_pages.reshape(tok, width_m).astype(f32)
    local_mean = jnp.mean(x, axis=1)
    local_m2 = jnp.sum(jnp.square(x - local_mean[:, None]), axis=1)
    stats = lax.all_gather(jnp.stack([local_mean, local_m2]), "mlp", axis=0, tiled=False)
    mean = jnp.mean(stats[:, 0], axis=0)
    m2 = jnp.sum(stats[:, 1] + width_m * jnp.square(stats[:, 0] - mean[None, :]), axis=0)
    scale = lax.rsqrt(m2 / width + EPS)
    column = lax.axis_index("mlp") * width_m
    gain = lax.dynamic_slice_in_dim(ln_gain, column, width_m, 0)
    bias = lax.dynamic_slice_in_dim(ln_bias, column, width_m, 0)
    normed = ((x - mean[:, None]) * scale[:, None] * gain + bias).astype(bf16)

    col_adapter = jnp.arange(NAD * R) // R
    fold = (jnp.arange(NAD * R)[:, None] % R == jnp.arange(R)[None, :]).astype(bf16)
    held_mask = held_adapter[:, None] == col_adapter[None, :]

    def pick(down):
        return mm(jnp.where(held_mask, mm(normed, down), 0.0).astype(bf16), fold)

    picked = jnp.concatenate([pick(down_query), pick(down_value), pick(down_fc)], axis=1)
    pad = 128
    picked = jnp.pad(picked.astype(bf16), ((0, 0), (0, pad - 3 * R)))

    per = groups // lanes
    part = tok // lanes
    pieces = normed.reshape(lanes, part, per, chunk).transpose(2, 0, 1, 3)
    everyone, picks = spread_rows(pieces, picked, groups, lanes)
    ordered = mm(perm_low, everyone.reshape(pages, page_len * chunk)).astype(bf16)
    ordered = ordered.reshape(groups, tok, chunk)

    held_chosen = jnp.sum(picks.astype(f32), axis=0).astype(bf16)
    held_perm = lax.dynamic_slice_in_dim(perm_low, me * pg_dev, pg_dev, 1)
    placed = mm(held_perm, held_chosen.reshape(pg_dev, page_len * pad)).astype(bf16)
    placed = placed.reshape(groups, tok, pad)
    own_mask = adapter[:, None] == col_adapter[None, :]

    def lift(low, up):
        wide = mm(low, fold.T).astype(bf16)
        return mm(jnp.where(own_mask, wide, jnp.zeros((), bf16)), up)

    total = 3 * heads_w + ff
    w_in = jnp.concatenate([w_query, w_key, w_value, w_fc_in], axis=1)
    if groups <= 8:
        w_tiles = w_in.reshape(chunk, total // TILE, TILE).transpose(1, 0, 2)
        base, chosen = reduce_rows(ordered, w_tiles, placed)
        base = base.transpose(1, 0, 2).reshape(tok, total)
    else:
        part_sum = mm(ordered.reshape(groups * tok, chunk), w_in).astype(bf16)
        part_sum = part_sum.reshape(groups, tok, total)
        base = lax.psum_scatter(part_sum, "req", scatter_dimension=0, tiled=False).astype(f32)
        chosen = lax.psum_scatter(placed, "req", scatter_dimension=0, tiled=False)

    row_iota = jnp.arange(tok)
    start = jnp.sum((request_id[None, :] < request_id[:, None]).astype(jnp.int32), axis=1)
    pos = row_iota - start
    mask = (request_id[:, None] == request_id[None, :]) & (row_iota[None, :] <= row_iota[:, None])
    query = base[:, :heads_w] + lift(chosen[:, :R], up_query)
    query = rotate_flat(query, pos).astype(bf16).reshape(tok, heads_w // HS, HS)
    keys = rotate_flat(base[:, heads_w : 2 * heads_w], pos).astype(bf16)
    keys = keys.reshape(tok, heads_w // HS, HS)
    value = base[:, 2 * heads_w : 3 * heads_w] + lift(chosen[:, R : 2 * R], up_value)
    value = value.astype(bf16).reshape(tok, heads_w // HS, HS)
    scores = jnp.einsum("qhd,khd->hqk", query, keys, preferred_element_type=f32) * HS ** (-0.5)
    scores = jnp.where(mask[None, :, :], scores, -1e30)
    top = jnp.max(scores, axis=2, keepdims=True)
    weights = jnp.exp(scores - top)
    probs = (weights / jnp.sum(weights, axis=2, keepdims=True)).astype(bf16)
    attn = jnp.einsum("hqk,khd->qhd", probs, value, preferred_element_type=f32)
    attn = attn.astype(bf16).reshape(tok, heads_w)
    hidden = gelu_tanh(base[:, 3 * heads_w :] + lift(chosen[:, 2 * R : 3 * R], up_fc) + b_fc_in)
    act = jnp.concatenate([attn, hidden.astype(bf16)], axis=1)

    w_out = jnp.concatenate([w_attn_out, w_fc_out], axis=0)
    if groups <= 8:
        tiles = (heads_w + ff) // TILE
        act = act.reshape(tok, tiles, TILE).transpose(1, 0, 2)
        out = gather_multiply(act, w_out.reshape(tiles, TILE, chunk), groups)
    else:
        acts = lax.all_gather(act, "req", axis=0, tiled=False)
        out = mm(acts.reshape(groups * tok, heads_w + ff), w_out).astype(bf16)
    out = mm(perm_low.T, out.reshape(pages, page_len * chunk)).astype(bf16)
    shares = collect_rows(out.reshape(groups, lanes, part, chunk))
    shares = shares.transpose(1, 2, 0, 3).reshape(tok, width_m)
    result = (x + shares.astype(f32) + b_fc_out).astype(bf16)
    return result.reshape(pg_dev, page_len, width_m)


def solution(mesh):
    in_specs = (
        P("req", None, "mlp"),
        P("req"),
        P("req"),
        P("req"),
        P(),
        P(),
        P("req", "mlp"),
        P("req", "mlp"),
        P("req", "mlp"),
        P("mlp", "req"),
        P("mlp", None),
        P(None, "mlp"),
        P("mlp", None),
        P(None, "mlp"),
        P("req", "mlp"),
        P("mlp"),
        P("mlp", None),
        P(None, "mlp"),
        P("mlp", "req"),
        P("mlp"),
    )
    out_specs = P("req", None, "mlp")
    return jax.shard_map(
        on_device, mesh=mesh, in_specs=in_specs, out_specs=out_specs, check_vma=False
    )
```

```python
import functools

import jax
import jax.numpy as jnp
from jax import lax
from jax.experimental import pallas as pl
from jax.experimental.pallas import tpu as pltpu
from jax.sharding import PartitionSpec as P

HS = 256
ROT = 64
NAD = 64
R = 16
EPS = 1e-05

bf16 = jnp.bfloat16
f32 = jnp.float32


def mm(a, b):
    return jnp.dot(a, b, preferred_element_type=f32)


def gelu_tanh(v):
    return 0.5 * v * (1.0 + jnp.tanh(0.7978845608028654 * (v + 0.044715 * v * v * v)))


def rotate_flat(block, pos):
    cols = block.shape[1]
    within = jnp.arange(cols) % HS
    turned = within < ROT
    freq = jnp.power(10000.0, -(within // 2).astype(f32) * 2.0 / ROT)
    angle = jnp.where(turned[None, :], pos.astype(f32)[:, None] * freq[None, :], 0.0)
    even = (within % 2 == 0)[None, :]
    other = jnp.where(even, -jnp.roll(block, -1, axis=1), jnp.roll(block, 1, axis=1))
    return jnp.where(turned[None, :], block * jnp.cos(angle) + other * jnp.sin(angle), block)


MESH = pl.DeviceIdType.MESH
VM = pl.BlockSpec(memory_space=pltpu.VMEM)
ANY = pl.BlockSpec(memory_space=pl.ANY)
TILE = 512


def params(collective_id, mib):
    return pltpu.CompilerParams(
        collective_id=collective_id, has_side_effects=True, vmem_limit_bytes=mib << 20
    )


def signal(barrier, target):
    pl.semaphore_signal(barrier, inc=1, device_id=target, device_id_type=MESH)


def ring_place(index, n):
    turn, height = index % 2, index // 2
    return height + turn * (n - 1 - 2 * height)


def ring_index(place, n):
    turn = place // (n // 2)
    return 2 * (place + turn * (n - 1 - 2 * place)) + turn


def ring_ids(n):
    place = ring_place(lax.axis_index("req"), n)
    lane = lax.axis_index("mlp")
    right = (ring_index((place + 1) % n, n), lane)
    left = (ring_index((place + n - 1) % n, n), lane)
    return place, (right, left)


def ring_barrier(targets):
    barrier = pltpu.get_barrier_semaphore()
    for target in targets:
        signal(barrier, target)
    pl.semaphore_wait(barrier, 2)


def greet_kernel(n, lanes, int_ref, stat_ref, ints_ref, stats_ref, isend, irecv, ssend, srecv):
    me, lane = lax.axis_index("req"), lax.axis_index("mlp")
    barrier = pltpu.get_barrier_semaphore()

    @pl.loop(1, n)
    def _(k):
        signal(barrier, ((me + k) % n, lane))

    for k in range(1, lanes):
        signal(barrier, (me, (lane + k) % lanes))
    pl.semaphore_wait(barrier, n + lanes - 2)

    def move(src, dst, send, recv, k, slot, target):
        return pltpu.make_async_remote_copy(
            src_ref=src,
            dst_ref=dst.at[slot],
            send_sem=send.at[k],
            recv_sem=recv.at[slot],
            device_id=target,
            device_id_type=MESH,
        )

    def along_req(k, slot):
        return move(int_ref, ints_ref, isend, irecv, k, slot, ((me + k) % n, lane))

    def along_mlp(k, slot):
        return move(stat_ref, stats_ref, ssend, srecv, k, slot, (me, (lane + k) % lanes))

    for k in range(1, lanes):
        along_mlp(k, lane).start()

    @pl.loop(1, n)
    def _(k):
        along_req(k, me).start()

    ints_ref[me] = int_ref[...]
    stats_ref[lane] = stat_ref[...]
    for k in range(1, lanes):
        along_mlp(k, (lane + k) % lanes).wait_recv()
        along_mlp(k, lane).wait_send()

    @pl.loop(1, n)
    def _(k):
        along_req(k, (me + k) % n).wait_recv()
        along_req(k, me).wait_send()


def greet(ints, stats, n, lanes):
    return pl.pallas_call(
        functools.partial(greet_kernel, n, lanes),
        out_shape=(
            jax.ShapeDtypeStruct((n,) + ints.shape, jnp.int32),
            jax.ShapeDtypeStruct((lanes,) + stats.shape, f32),
        ),
        in_specs=[VM] * 2,
        out_specs=(VM, VM),
        scratch_shapes=[
            pltpu.SemaphoreType.DMA((n,)),
            pltpu.SemaphoreType.DMA((n,)),
            pltpu.SemaphoreType.DMA((lanes,)),
            pltpu.SemaphoreType.DMA((lanes,)),
        ],
        compiler_params=params(5, 16),
        name="greet",
    )(ints, stats)


def columns(t):
    return pl.ds(pl.multiple_of(t * TILE, TILE), TILE)


def reduce_kernel(
    n, x_ref, wq_ref, wk_ref, wv_ref, wf_ref, extra_ref, sum_ref, esum_ref,
    w_ref, first, got, egot, sends, recvs, loads,
):
    half = n // 2
    tiles = w_ref.shape[0]
    pieces = []
    for ref in (wq_ref, wk_ref, wv_ref, wf_ref):
        for c in range(ref.shape[1] // TILE):
            t = len(pieces)
            src = ref.at[:, pl.ds(c * TILE, TILE)]
            pieces.append(pltpu.make_async_copy(src, w_ref.at[t], loads.at[t]))
            pieces[-1].start()
    rows = x_ref.shape[1]
    mid = rows // 2
    place, targets = ring_ids(n)
    ring_barrier(targets)
    spans = (pl.ds(0, mid), pl.ds(mid, mid))

    def owner(side, step):
        away = half - step if side == 0 else n - half + step
        return ring_index((place + away) % n, n)

    def own(index, t):
        return mm(x_ref[index], w_ref[t])

    def move(side, step, t, extra=False):
        slot = tiles if extra else t
        buffer = egot if extra else got
        if step == 0:
            src = buffer.at[2 * half, spans[side]] if extra else first.at[t, spans[side]]
            at = (side * half, spans[side])
        else:
            at = (side * half + step,)
            src = buffer.at[side * half + step - 1] if extra else got.at[side * half + step - 1, t]
        if not extra:
            at = (at[0], t) + at[1:]
        return pltpu.make_async_remote_copy(
            src_ref=src,
            dst_ref=buffer.at[at],
            send_sem=sends.at[side * half + step, slot],
            recv_sem=recvs.at[side * half + step, slot],
            device_id=targets[side],
            device_id_type=MESH,
        )

    egot[2 * half] = extra_ref[owner(0, 0)]
    for side in (0, 1):
        move(side, 0, 0, True).start()
    for piece in pieces:
        piece.wait()

    @pl.loop(0, tiles)
    def _(t):
        first[t] = own(owner(0, 0), t).astype(bf16)
        for side in (0, 1):
            move(side, 0, t).start()

    for step in range(1, half):
        for side in (0, 1):
            slot = side * half + step - 1
            mine = extra_ref[owner(side, step)]
            move(side, step - 1, 0, True).wait_recv()
            if step == 1:
                egot[slot, spans[side]] += mine[side * mid : side * mid + mid]
                egot[slot, spans[1 - side]] = mine[(1 - side) * mid : (1 - side) * mid + mid]
            else:
                egot[slot] += mine
            move(side, step, 0, True).start()

        @pl.loop(0, tiles)
        def _(t):
            for side in (0, 1):
                slot = side * half + step - 1
                mine = own(owner(side, step), t)
                move(side, step - 1, t).wait_recv()
                if step == 1:
                    a = mine[side * mid : side * mid + mid]
                    b = mine[(1 - side) * mid : (1 - side) * mid + mid]
                    here = got[slot, t, spans[side]].astype(f32)
                    got[slot, t, spans[side]] = (here + a).astype(bf16)
                    got[slot, t, spans[1 - side]] = b.astype(bf16)
                else:
                    got[slot, t] = (got[slot, t].astype(f32) + mine).astype(bf16)
                move(side, step, t).start()

    for side in (0, 1):
        move(side, half - 1, 0, True).wait_recv()
    me = lax.axis_index("req")
    esum_ref[...] = extra_ref[me] + egot[half - 1] + egot[2 * half - 1]

    @pl.loop(0, tiles)
    def _(t):
        mine = own(me, t)
        for side in (0, 1):
            move(side, half - 1, t).wait_recv()
        sum_ref[:, columns(t)] = mine + got[half - 1, t].astype(f32) + got[2 * half - 1, t].astype(f32)

    for step in range(half):
        for side in (0, 1):
            move(side, step, 0, True).wait_send()

        @pl.loop(0, tiles)
        def _(t):
            for side in (0, 1):
                move(side, step, t).wait_send()


def reduce_rows(x, weights, extra):
    n, rows, depth = x.shape
    tiles = sum(w.shape[1] for w in weights) // TILE
    pad = extra.shape[2]
    return pl.pallas_call(
        functools.partial(reduce_kernel, n),
        out_shape=(
            jax.ShapeDtypeStruct((rows, tiles * TILE), f32),
            jax.ShapeDtypeStruct((rows, pad), bf16),
        ),
        in_specs=[VM] + [ANY] * 4 + [VM],
        out_specs=(VM, VM),
        scratch_shapes=[
            pltpu.VMEM((tiles, depth, TILE), bf16),
            pltpu.VMEM((tiles, rows, TILE), bf16),
            pltpu.VMEM((n, tiles, rows, TILE), bf16),
            pltpu.VMEM((n + 1, rows, pad), bf16),
            pltpu.SemaphoreType.DMA((n, tiles + 1)),
            pltpu.SemaphoreType.DMA((n, tiles + 1)),
            pltpu.SemaphoreType.DMA((tiles,)),
        ],
        compiler_params=params(1, 48),
        name="reduce_rows",
    )(x, *weights, extra)


def gather_kernel(n, act_ref, wa_ref, wf_ref, out_ref, w_ref, got, total, sends, recvs, loads):
    half = n // 2
    tiles = w_ref.shape[0]
    rows = act_ref.shape[0]
    pieces = []
    for ref in (wa_ref, wf_ref):
        for c in range(ref.shape[0] // TILE):
            t = len(pieces)
            src = ref.at[pl.ds(c * TILE, TILE)]
            pieces.append(pltpu.make_async_copy(src, w_ref.at[t], loads.at[t]))
            pieces[-1].start()
    mid = rows // 2
    place, targets = ring_ids(n)
    ring_barrier(targets)
    spans = (pl.ds(0, mid), pl.ds(mid, mid))

    def move(side, step, t):
        src = act_ref.at[:, columns(t)] if step == 0 else got.at[side * half + step - 1, t]
        dst = got.at[side * half + step, t]
        if step == half - 1:
            dst = got.at[half - 1, t, spans[side]]
            src = src.at[spans[side]]
        return pltpu.make_async_remote_copy(
            src_ref=src,
            dst_ref=dst,
            send_sem=sends.at[side * half + step, t],
            recv_sem=recvs.at[side * half + step, t],
            device_id=targets[side],
            device_id_type=MESH,
        )

    @pl.loop(0, tiles)
    def _(t):
        for side in (0, 1):
            move(side, 0, t).start()

    total[...] = jnp.zeros_like(total)
    for piece in pieces:
        piece.wait()

    @pl.loop(0, tiles)
    def _(t):
        total[0] += mm(act_ref[:, columns(t)], w_ref[t])

    out_ref[lax.axis_index("req")] = total[0].astype(bf16)

    for step in range(1, half):
        total[...] = jnp.zeros_like(total)

        @pl.loop(0, tiles)
        def _(t):
            for side in (0, 1):
                move(side, step - 1, t).wait_recv()
                move(side, step, t).start()
            for side in (0, 1):
                total[side] += mm(got[side * half + step - 1, t], w_ref[t])

        for side in (0, 1):
            away = n - step if side == 0 else step
            out_ref[ring_index((place + away) % n, n)] = total[side].astype(bf16)

    total[...] = jnp.zeros_like(total)

    @pl.loop(0, tiles)
    def _(t):
        for side in (0, 1):
            move(side, half - 1, t).wait_recv()
        total[0] += mm(got[half - 1, t], w_ref[t])

    out_ref[ring_index((place + half) % n, n)] = total[0].astype(bf16)

    for step in range(half):

        @pl.loop(0, tiles)
        def _(t):
            for side in (0, 1):
                move(side, step, t).wait_send()


def gather_multiply(act, weights, n):
    rows, depth = act.shape
    tiles = depth // TILE
    width = weights[0].shape[1]
    return pl.pallas_call(
        functools.partial(gather_kernel, n),
        out_shape=jax.ShapeDtypeStruct((n, rows, width), bf16),
        in_specs=[VM, ANY, ANY],
        out_specs=VM,
        scratch_shapes=[
            pltpu.VMEM((tiles, TILE, width), bf16),
            pltpu.VMEM((n, tiles, rows, TILE), bf16),
            pltpu.VMEM((2, rows, width), f32),
            pltpu.SemaphoreType.DMA((n, tiles)),
            pltpu.SemaphoreType.DMA((n, tiles)),
            pltpu.SemaphoreType.DMA((tiles,)),
        ],
        compiler_params=params(2, 48),
        name="gather_multiply",
    )(act, *weights)


def exchange_barrier(n, lanes):
    me, lane = lax.axis_index("req"), lax.axis_index("mlp")
    per = n // lanes
    alone = jnp.where(me // per == lane, 1, 0)
    barrier = pltpu.get_barrier_semaphore()
    for k in range(1, lanes):
        signal(barrier, (me, (lane + k) % lanes))

    @pl.loop(0, n)
    def _(i):
        there, t = lane * per + i // lanes, i % lanes

        @pl.when((there != me) | (t != lane))
        def _():
            signal(barrier, (there, t))

        @pl.when((i != me) | (me // per != lane))
        def _():
            signal(barrier, (i, me // per))

    pl.semaphore_wait(barrier, lanes - 1 + 2 * (n - alone))


def spread_kernel(n, lanes, x_ref, pick_ref, all_ref, picks_ref, sends, recvs, msends, mrecvs, ps, pr):
    me, lane = lax.axis_index("req"), lax.axis_index("mlp")
    per = n // lanes
    exchange_barrier(n, lanes)

    def out_move(j, t, source):
        return pltpu.make_async_remote_copy(
            src_ref=x_ref.at[j, t],
            dst_ref=all_ref.at[source, t],
            send_sem=sends.at[j, t],
            recv_sem=recvs.at[source],
            device_id=(lane * per + j, t),
            device_id_type=MESH,
        )

    def in_move(source):
        return pltpu.make_async_remote_copy(
            src_ref=x_ref.at[0, lane],
            dst_ref=all_ref.at[source, lane],
            send_sem=sends.at[0, lane],
            recv_sem=recvs.at[source],
            device_id=(source, me // per),
            device_id_type=MESH,
        )

    def fan(k, source, t):
        return pltpu.make_async_remote_copy(
            src_ref=all_ref.at[source, t],
            dst_ref=all_ref.at[source, t],
            send_sem=msends.at[k, source],
            recv_sem=mrecvs.at[t, source],
            device_id=(me, (lane + k) % lanes),
            device_id_type=MESH,
        )

    def share(k, t):
        return pltpu.make_async_remote_copy(
            src_ref=pick_ref,
            dst_ref=picks_ref.at[t],
            send_sem=ps.at[k],
            recv_sem=pr.at[t],
            device_id=(me, (lane + k) % lanes),
            device_id_type=MESH,
        )

    @pl.loop(0, n)
    def _(i):
        j, t = i // lanes, i % lanes
        self = (lane * per + j == me) & (t == lane)

        @pl.when(jnp.logical_not(self))
        def _():
            out_move(j, t, me).start()

        @pl.when(self)
        def _():
            all_ref[me, lane] = x_ref[j, t]

    for k in range(1, lanes):
        share(k, lane).start()
    picks_ref[lane] = pick_ref[...]

    @pl.loop(0, n)
    def _(i):
        source = (me + i) % n

        @pl.when((source != me) | (me // per != lane))
        def _():
            in_move(source).wait_recv()

        for k in range(1, lanes):
            fan(k, source, lane).start()

    @pl.loop(0, n)
    def _(source):
        for k in range(1, lanes):
            fan(k, source, (lane + k) % lanes).wait_recv()

    for k in range(1, lanes):
        share(k, (lane + k) % lanes).wait_recv()
        share(k, lane).wait_send()

    @pl.loop(0, n)
    def _(i):
        j, t = i // lanes, i % lanes

        @pl.when((lane * per + j != me) | (t != lane))
        def _():
            out_move(j, t, me).wait_send()

        for k in range(1, lanes):
            fan(k, i, lane).wait_send()


def spread_rows(x, picked, n, lanes):
    _, _, part, chunk = x.shape
    return pl.pallas_call(
        functools.partial(spread_kernel, n, lanes),
        out_shape=(
            jax.ShapeDtypeStruct((n, lanes, part, chunk), bf16),
            jax.ShapeDtypeStruct((lanes,) + picked.shape, bf16),
        ),
        in_specs=[VM] * 2,
        out_specs=(VM, VM),
        scratch_shapes=[
            pltpu.SemaphoreType.DMA((n // lanes, lanes)),
            pltpu.SemaphoreType.DMA((n,)),
            pltpu.SemaphoreType.DMA((lanes, n)),
            pltpu.SemaphoreType.DMA((lanes, n)),
            pltpu.SemaphoreType.DMA((lanes,)),
            pltpu.SemaphoreType.DMA((lanes,)),
        ],
        compiler_params=params(3, 24),
        name="spread_rows",
    )(x, picked)


def collect_kernel(n, lanes, y_ref, out_ref, part, ready, msends, mrecvs, sends, recvs):
    me, lane = lax.axis_index("req"), lax.axis_index("mlp")
    per = n // lanes
    exchange_barrier(n, lanes)

    def cross(k, d):
        return pltpu.make_async_remote_copy(
            src_ref=y_ref.at[d, (lane + k) % lanes],
            dst_ref=part.at[k - 1, d],
            send_sem=msends.at[k - 1, d],
            recv_sem=mrecvs.at[k - 1, d],
            device_id=(me, (lane + k) % lanes),
            device_id_type=MESH,
        )

    def home(d):
        return pltpu.make_async_remote_copy(
            src_ref=ready.at[d],
            dst_ref=out_ref.at[me % per, lane],
            send_sem=sends.at[d],
            recv_sem=recvs.at[me % per, lane],
            device_id=(d, me // per),
            device_id_type=MESH,
        )

    def arrive(j, t):
        return pltpu.make_async_remote_copy(
            src_ref=ready.at[0],
            dst_ref=out_ref.at[j, t],
            send_sem=sends.at[0],
            recv_sem=recvs.at[j, t],
            device_id=(lane * per + j, t),
            device_id_type=MESH,
        )

    @pl.loop(0, n)
    def _(i):
        for k in range(1, lanes):
            cross(k, (me + i) % n).start()

    @pl.loop(0, n)
    def _(i):
        d = (me + i) % n
        total = y_ref[d, lane].astype(f32)
        for k in range(1, lanes):
            cross(k, d).wait_recv()
            total += part[k - 1, d].astype(f32)
        ready[d] = total.astype(bf16)
        self = (d == me) & (me // per == lane)

        @pl.when(jnp.logical_not(self))
        def _():
            home(d).start()

        @pl.when(self)
        def _():
            out_ref[me % per, lane] = total.astype(bf16)

    @pl.loop(0, n)
    def _(i):
        j, t = i // lanes, i % lanes

        @pl.when((lane * per + j != me) | (t != lane))
        def _():
            arrive(j, t).wait_recv()

        @pl.when((i != me) | (me // per != lane))
        def _():
            home(i).wait_send()

        for k in range(1, lanes):
            cross(k, i).wait_send()


def collect_rows(y):
    n, lanes, rows, chunk = y.shape
    per = n // lanes
    return pl.pallas_call(
        functools.partial(collect_kernel, n, lanes),
        out_shape=jax.ShapeDtypeStruct((per, lanes, rows, chunk), bf16),
        in_specs=[VM],
        out_specs=VM,
        scratch_shapes=[
            pltpu.VMEM((lanes - 1, n, rows, chunk), bf16),
            pltpu.VMEM((n, rows, chunk), bf16),
            pltpu.SemaphoreType.DMA((lanes - 1, n)),
            pltpu.SemaphoreType.DMA((lanes - 1, n)),
            pltpu.SemaphoreType.DMA((n,)),
            pltpu.SemaphoreType.DMA((per, lanes)),
        ],
        compiler_params=params(4, 24),
        name="collect_rows",
    )(y)


def on_device(
    x_pages,
    page_owner,
    request_id,
    adapter_table,
    ln_gain,
    ln_bias,
    w_query,
    w_key,
    w_value,
    w_attn_out,
    down_query,
    up_query,
    down_value,
    up_value,
    w_fc_in,
    b_fc_in,
    down_fc,
    up_fc,
    w_fc_out,
    b_fc_out,
):
    groups = lax.axis_size("req")
    lanes = lax.axis_size("mlp")
    me = lax.axis_index("req")
    pg_dev, page_len, width_m = x_pages.shape
    pages = groups * pg_dev
    tok = request_id.shape[0]
    width = width_m * lanes
    chunk = w_query.shape[0]
    heads_w = w_query.shape[1]
    ff = w_fc_in.shape[1]

    local_req = request_id - me * tok
    lookup = local_req[:, None] == jnp.arange(tok)[None, :]
    adapter = jnp.sum(jnp.where(lookup, adapter_table[None, :], 0), axis=1)
    x = x_pages.reshape(tok, width_m).astype(f32)
    local_mean = jnp.mean(x, axis=1)
    local_m2 = jnp.sum(jnp.square(x - local_mean[:, None]), axis=1)
    numbers = jnp.concatenate([page_owner, adapter])
    count = pg_dev + tok
    room = -(-count // 1024) * 1024
    numbers = jnp.pad(numbers, (0, room - count)).reshape(room // 128, 128)
    local = jnp.pad(jnp.stack([local_mean, local_m2]), ((0, 6), (0, 0)))
    ints, stats = greet(numbers, local, groups, lanes)
    ints = ints.reshape(groups, room)
    owner_all = ints[:, :pg_dev].reshape(pages)
    adapter_all = ints[:, pg_dev:count].reshape(pages, page_len)
    iota = jnp.arange(pages)
    earlier = (owner_all[None, :] == owner_all[:, None]) & (iota[None, :] < iota[:, None])
    dest = owner_all * pg_dev + jnp.sum(earlier.astype(jnp.int32), axis=1)
    perm = dest[None, :] == iota[:, None]
    perm_low = perm.astype(bf16)
    mine = lax.dynamic_slice_in_dim(dest, me * pg_dev, pg_dev, 0)
    held_adapter = jnp.sum(
        jnp.where((mine[:, None] == iota[None, :])[:, :, None], adapter_all[None, :, :], 0), axis=1
    ).reshape(tok)

    mean = jnp.mean(stats[:, 0], axis=0)
    m2 = jnp.sum(stats[:, 1] + width_m * jnp.square(stats[:, 0] - mean[None, :]), axis=0)
    scale = lax.rsqrt(m2 / width + EPS)
    column = lax.axis_index("mlp") * width_m
    gain = lax.dynamic_slice_in_dim(ln_gain, column, width_m, 0)
    bias = lax.dynamic_slice_in_dim(ln_bias, column, width_m, 0)
    normed = ((x - mean[:, None]) * scale[:, None] * gain + bias).astype(bf16)

    col_adapter = jnp.arange(NAD * R) // R
    fold = (jnp.arange(NAD * R)[:, None] % R == jnp.arange(R)[None, :]).astype(bf16)
    held_mask = held_adapter[:, None] == col_adapter[None, :]

    def pick(down):
        return mm(jnp.where(held_mask, mm(normed, down), 0.0).astype(bf16), fold)

    picked = jnp.concatenate([pick(down_query), pick(down_value), pick(down_fc)], axis=1)
    pad = 128
    picked = jnp.pad(picked.astype(bf16), ((0, 0), (0, pad - 3 * R)))

    per = groups // lanes
    part = tok // lanes
    pieces = normed.reshape(lanes, part, per, chunk).transpose(2, 0, 1, 3)
    everyone, picks = spread_rows(pieces, picked, groups, lanes)
    ordered = mm(perm_low, everyone.reshape(pages, page_len * chunk)).astype(bf16)
    ordered = ordered.reshape(groups, tok, chunk)

    held_chosen = jnp.sum(picks.astype(f32), axis=0).astype(bf16)
    held_perm = lax.dynamic_slice_in_dim(perm_low, me * pg_dev, pg_dev, 1)
    placed = mm(held_perm, held_chosen.reshape(pg_dev, page_len * pad)).astype(bf16)
    placed = placed.reshape(groups, tok, pad)
    own_mask = adapter[:, None] == col_adapter[None, :]

    def lift(low, up):
        wide = mm(low, fold.T).astype(bf16)
        return mm(jnp.where(own_mask, wide, jnp.zeros((), bf16)), up)

    total = 3 * heads_w + ff
    if groups <= 8:
        base, chosen = reduce_rows(ordered, (w_query, w_key, w_value, w_fc_in), placed)
    else:
        w_in = jnp.concatenate([w_query, w_key, w_value, w_fc_in], axis=1)
        part_sum = mm(ordered.reshape(groups * tok, chunk), w_in).astype(bf16)
        part_sum = part_sum.reshape(groups, tok, total)
        base = lax.psum_scatter(part_sum, "req", scatter_dimension=0, tiled=False).astype(f32)
        chosen = lax.psum_scatter(placed, "req", scatter_dimension=0, tiled=False)

    row_iota = jnp.arange(tok)
    start = jnp.sum((request_id[None, :] < request_id[:, None]).astype(jnp.int32), axis=1)
    pos = row_iota - start
    mask = (request_id[:, None] == request_id[None, :]) & (row_iota[None, :] <= row_iota[:, None])
    query = base[:, :heads_w] + lift(chosen[:, :R], up_query)
    query = rotate_flat(query, pos).astype(bf16).reshape(tok, heads_w // HS, HS)
    keys = rotate_flat(base[:, heads_w : 2 * heads_w], pos).astype(bf16)
    keys = keys.reshape(tok, heads_w // HS, HS)
    value = base[:, 2 * heads_w : 3 * heads_w] + lift(chosen[:, R : 2 * R], up_value)
    value = value.astype(bf16).reshape(tok, heads_w // HS, HS)
    scores = jnp.einsum("qhd,khd->hqk", query, keys, preferred_element_type=f32) * HS ** (-0.5)
    scores = jnp.where(mask[None, :, :], scores, -1e30)
    top = jnp.max(scores, axis=2, keepdims=True)
    weights = jnp.exp(scores - top)
    probs = (weights / jnp.sum(weights, axis=2, keepdims=True)).astype(bf16)
    attn = jnp.einsum("hqk,khd->qhd", probs, value, preferred_element_type=f32)
    attn = attn.astype(bf16).reshape(tok, heads_w)
    hidden = gelu_tanh(base[:, 3 * heads_w :] + lift(chosen[:, 2 * R : 3 * R], up_fc) + b_fc_in)
    act = jnp.concatenate([attn, hidden.astype(bf16)], axis=1)

    if groups <= 8:
        out = gather_multiply(act, (w_attn_out, w_fc_out), groups)
    else:
        w_out = jnp.concatenate([w_attn_out, w_fc_out], axis=0)
        acts = lax.all_gather(act, "req", axis=0, tiled=False)
        out = mm(acts.reshape(groups * tok, heads_w + ff), w_out).astype(bf16)
    out = mm(perm_low.T, out.reshape(pages, page_len * chunk)).astype(bf16)
    shares = collect_rows(out.reshape(groups, lanes, part, chunk))
    shares = shares.transpose(1, 2, 0, 3).reshape(tok, width_m)
    result = (x + shares.astype(f32) + b_fc_out).astype(bf16)
    return result.reshape(pg_dev, page_len, width_m)


def solution(mesh):
    in_specs = (
        P("req", None, "mlp"),
        P("req"),
        P("req"),
        P("req"),
        P(),
        P(),
        P("req", "mlp"),
        P("req", "mlp"),
        P("req", "mlp"),
        P("mlp", "req"),
        P("mlp", None),
        P(None, "mlp"),
        P("mlp", None),
        P(None, "mlp"),
        P("req", "mlp"),
        P("mlp"),
        P("mlp", None),
        P(None, "mlp"),
        P("mlp", "req"),
        P("mlp"),
    )
    out_specs = P("req", None, "mlp")
    return jax.shard_map(
        on_device, mesh=mesh, in_specs=in_specs, out_specs=out_specs, check_vma=False
    )
```
